32 devices in a mesh: seq: 4 (over z), head: 4 (over y, core), req: 2 (over x).
Axes of the slice: x: 2, y: 2, z: 4, core: 2. Of those that a mesh axis runs over, the one named last changes fastest.
Arguments:
- pre_qkv: bfloat16 [8192, 3, 4096], P('seq', None, ('head', 'req')), may hold values from -200 to 200
- cache_kv: bfloat16 [8, 2, 256, 4096], P('req', None, 'seq', 'head'), may hold values from -6 to 6
- dec_new: bfloat16 [16, 3, 2, 4096], P('req', None, None, 'head'), may hold values from -200 to 200
- out_weight: bfloat16 [4096, 4096], P('head', 'seq'), may hold values from -0.09375 to 0.09375
- owner_slot: int32 [8], replicated, may hold values from 0 to 15, as said below
- prompt_lengths: int32 [8], replicated, may hold values from 1 to 256
Outputs:
- prefill_out: bfloat16 [8192, 4096], P('seq', ('head', 'req'))
- decode_out: bfloat16 [16, 2, 4096], P('req', None, ('seq', 'head'))
The draws below stay inside these ranges and needn't reach their ends.
Inputs may be any that keep to these rules, and one draw needn't show every extreme that they name: `owner_slot`: distinct slots; slot s belongs to decode group s // 8. Of the requests of one aligned block of 4, at most 4 are owned by one group, and the last group, 1, owns exactly 4 from every block.
All inputs are finite; a program needn't handle non-finite values.
Results may differ from the reference program's by a relative error of at most 0.012.
Values may be sent and summed in bfloat16 or wider, within the bound.
A program may use at most 128 MiB of HBM per device.

```python
from functools import reduce
import jax
import jax.numpy as jnp
from jax import lax

D = 4096
HEADS = 32
HEAD_DIM = 128
TOK_DEV = 2048
REQ_DEV = 4
GROUPS = 2
STRETCH = 8192
FAR_STRIDE = 4
REQS = 8
SLOT_DEV = 8
SLOTS = 16
CAPACITY = 4
CACHE = 256


def owner_table(key):
    base_key = jax.random.fold_in(key, 7)
    busy_group = GROUPS - 1
    tickets = jnp.arange(GROUPS * CAPACITY)
    ticket_group = tickets // CAPACITY

    def one_block(block_index):
        block_key = jax.random.fold_in(base_key, 100 + block_index)
        order_ints = jax.random.permutation(jax.random.fold_in(block_key, 1), GROUPS * CAPACITY)
        ticket_score = jnp.where(ticket_group == busy_group, -1, order_ints)
        chosen = jnp.argsort(ticket_score, stable=True)[:REQ_DEV]
        return jax.random.permutation(jax.random.fold_in(block_key, 2), chosen)
    picked = jax.vmap(one_block)(jnp.arange(GROUPS))

    def seat_order(group_index):
        return jax.random.permutation(jax.random.fold_in(base_key, 5000 + group_index), SLOT_DEV)
    seat_orders = jax.vmap(seat_order)(jnp.arange(GROUPS))
    dest_group = picked // CAPACITY
    seat_index = picked % CAPACITY
    blocks = jnp.arange(GROUPS)[:, None]
    place_index = seat_orders[dest_group, blocks * CAPACITY + seat_index]
    return (dest_group * SLOT_DEV + place_index).reshape(REQS).astype(jnp.int32)


def cache_field(key):
    shape = (REQS, 2, CACHE, HEADS * HEAD_DIM)
    return jnp.clip(jax.random.normal(jax.random.fold_in(key, 11), shape, jnp.float32), -6.0, 6.0)


def draw_owner_slot(key, part):
    return owner_table(key)


def draw_cache_kv(key, part):
    return cache_field(key).astype(jnp.bfloat16)


def draw_dec_new(key, part):
    width = HEADS * HEAD_DIM
    fresh_rows = jnp.clip(jax.random.normal(jax.random.fold_in(key, 13), (SLOTS, 3, 2, width), jnp.float32), -6.0, 6.0)
    return fresh_rows.astype(jnp.bfloat16)


def draw_pre_qkv(key, part):
    width = HEADS * HEAD_DIM
    field = jnp.clip(jax.random.normal(jax.random.fold_in(key, 29), (STRETCH, 3, width), jnp.float32), -6.0, 6.0)
    return field.astype(jnp.bfloat16)


def set_ends(values, key, smallest, high):
    longest = values.shape.index(max(values.shape))
    spots = []
    for shift in (0, 1):
        where = [jax.random.randint(jax.random.fold_in(key, axis), (), 0, length) for axis, length in enumerate(values.shape)]
        where[longest] = (where[longest] + shift) % values.shape[longest]
        spots.append(tuple(where))
    return values.at[spots[0]].set(smallest).at[spots[1]].set(high)


def level_of(key, dims, split, least, high):
    def one(axis_at, blocks):
        heights = jax.random.uniform(jax.random.fold_in(jax.random.fold_in(key, 6), axis_at), (blocks,), jnp.float32, least / len(split), high / len(split))
        return jnp.repeat(jnp.exp(heights), dims[axis_at] // blocks).reshape((-1,) + (1,) * (len(dims) - axis_at - 1))

    loudness = one(*split[0])
    for cut in split[1:]:
        loudness = loudness * one(*cut)
    return loudness


def scatter_about(rng, shape, scale, most, cuts=(), kind=jnp.bfloat16):
    level = level_of(rng, shape, cuts, -0.22, 0.18) if cuts else 1.0
    values = jax.random.normal(rng, shape, jnp.float32) * scale * level
    return jnp.minimum(jnp.maximum(values, -most), most).astype(kind)


def setup_inputs(seed: int = 0) -> dict:
    key_of = jax.random.split(jax.random.key(seed), 7)
    return {
        "pre_qkv": draw_pre_qkv(jax.random.fold_in(key_of[6], 71), 0),
        "cache_kv": draw_cache_kv(jax.random.fold_in(key_of[6], 71), 0),
        "dec_new": draw_dec_new(jax.random.fold_in(key_of[6], 71), 0),
        "out_weight": scatter_about(key_of[3], (HEADS * HEAD_DIM, D), (HEADS * HEAD_DIM) ** -0.5, 0.09375, ((0, 4), (1, 4))),
        "owner_slot": draw_owner_slot(jax.random.fold_in(key_of[6], 71), 0),
        "prompt_lengths": set_ends(jax.random.randint(key_of[5], (REQS,), 1, CACHE + 1), jax.random.fold_in(key_of[5], 1), 1, CACHE).astype(jnp.int32),
    }


NEG_FILL = -1e30


def partial_block(query_rows, key_rows, value_rows, allowed):
    score_scale = query_rows.shape[-1] ** -0.5
    scores = jnp.einsum("qhd,khd->hqk", query_rows.astype(jnp.float32), key_rows.astype(jnp.float32)) * score_scale
    scores = jnp.where(allowed, scores, NEG_FILL)
    peak_score = jnp.max(scores, axis=-1)
    weights = jnp.where(allowed, jnp.exp(scores - peak_score[..., None]), 0.0)
    weight_sum = jnp.sum(weights, axis=-1)
    rounded = weights.astype(jnp.bfloat16).astype(jnp.float32)
    value_sum = jnp.einsum("hqk,khd->hqd", rounded, value_rows.astype(jnp.float32))
    return peak_score, weight_sum, value_sum


def combine_levels(levels):
    top_all = reduce(jnp.maximum, [level_term[0] for level_term in levels])
    numerator = 0.0
    denominator = 0.0
    for peak_score, weight_sum, value_sum in levels:
        factor = jnp.exp(peak_score - top_all)
        denominator = denominator + weight_sum * factor
        numerator = numerator + value_sum * factor[..., None]
    return numerator / denominator[..., None]


def prefill_head(packed):
    head_query, head_key, head_value, head_number = packed
    levels = []
    for span_rows, stride in ((TOK_DEV, 1), (4 * TOK_DEV, 4), (STRETCH, FAR_STRIDE)):
        residue = (head_number % stride).astype(jnp.int32)
        segments = STRETCH // span_rows
        sparse_count = span_rows // stride

        def sparse(field):
            shaped = field.reshape(segments, sparse_count, stride, HEAD_DIM)
            return jnp.take(shaped, residue, axis=2)

        allowed = jnp.arange(sparse_count)[None, :] <= jnp.arange(sparse_count)[:, None]

        def attend(parts):
            query_part, key_part, value_part = parts
            return partial_block(query_part[:, None], key_part[:, None], value_part[:, None], allowed)

        peak_score, weight_sum, value_sum = lax.map(attend, (sparse(head_query), sparse(head_key), sparse(head_value)))
        rows_level = STRETCH // stride
        peak_rows = jnp.full((rows_level, stride), NEG_FILL, jnp.float32).at[:, residue].set(peak_score.reshape(rows_level))
        sum_rows = jnp.zeros((rows_level, stride), jnp.float32).at[:, residue].set(weight_sum.reshape(rows_level))
        value_rows = jnp.zeros((rows_level, stride, HEAD_DIM), jnp.float32).at[:, residue].set(value_sum.reshape(rows_level, HEAD_DIM))
        levels.append((peak_rows.reshape(STRETCH), sum_rows.reshape(STRETCH), value_rows.reshape(STRETCH, HEAD_DIM)))
    return combine_levels(levels)


def reference(pre_qkv, cache_kv, dec_new, out_weight, owner_slot, prompt_lengths):
    def by_head(field):
        return jnp.swapaxes(field.reshape(STRETCH, HEADS, HEAD_DIM), 0, 1)

    attended = lax.map(prefill_head, (by_head(pre_qkv[:, 0]), by_head(pre_qkv[:, 1]), by_head(pre_qkv[:, 2]), jnp.arange(HEADS, dtype=jnp.int32)))
    prefill_out = jnp.swapaxes(attended, 0, 1).reshape(STRETCH, HEADS * HEAD_DIM).astype(jnp.bfloat16)

    def decode_one(packed):
        cache_rows, fresh_rows, length = packed
        query_rows = fresh_rows[0].reshape(2, HEADS, HEAD_DIM)
        new_keys = fresh_rows[1].reshape(2, HEADS, HEAD_DIM)
        new_values = fresh_rows[2].reshape(2, HEADS, HEAD_DIM)
        cache_keys = cache_rows[0].reshape(CACHE, HEADS, HEAD_DIM)
        cache_values = cache_rows[1].reshape(CACHE, HEADS, HEAD_DIM)
        allowed = jnp.broadcast_to(jnp.arange(CACHE)[None, :] < length, (2, CACHE))
        cached_term = partial_block(query_rows, cache_keys, cache_values, allowed)
        causal = jnp.arange(2)[None, :] <= jnp.arange(2)[:, None]
        fresh_term = partial_block(query_rows, new_keys, new_values, causal)
        mixed = combine_levels([cached_term, fresh_term])
        mixed_rows = jnp.swapaxes(mixed, 0, 1).reshape(2, HEADS * HEAD_DIM).astype(jnp.bfloat16)
        return jnp.dot(mixed_rows, out_weight, preferred_element_type=jnp.float32).astype(jnp.bfloat16)

    results = lax.map(decode_one, (cache_kv, dec_new[owner_slot], prompt_lengths))
    decode_out = jnp.zeros((SLOTS, 2, D), jnp.bfloat16).at[owner_slot].set(results)
    return prefill_out, decode_out
```

```python
import functools
from functools import reduce

import jax
import jax.numpy as jnp
from jax import lax
from jax.experimental import pallas as pl
from jax.experimental.pallas import tpu as pltpu
from jax.sharding import PartitionSpec as P

HEAD_DIM = 128
LOG2E = 1.4426950408889634


NEG_FILL = -1e30


def merged_2(value, axis, join):
    pieces = jax.tree.map(lambda part: lax.all_gather(part, axis), value)
    head = jax.tree.map(lambda part: part[0], pieces)
    tail = jax.tree.map(lambda part: part[1:], pieces)
    total, _ = lax.scan(lambda total, section: (join(total, section), None), head, tail)
    return total


def partial_block(query_rows, key_rows, value_rows, allowed):
    score_scale = query_rows.shape[-1] ** (-0.5)
    scores = (
        jnp.einsum("qhd,khd->hqk", query_rows, key_rows, preferred_element_type=jnp.float32)
        * score_scale
    )
    scores = jnp.where(allowed, scores, NEG_FILL)
    peak_score = jnp.max(scores, axis=-1)
    weights = jnp.where(allowed, jnp.exp(scores - peak_score[..., None]), 0.0)
    weight_sum = jnp.sum(weights, axis=-1)
    value_sum = jnp.einsum(
        "hqk,khd->hqd", weights.astype(jnp.bfloat16), value_rows, preferred_element_type=jnp.float32
    )
    return (peak_score, weight_sum, value_sum)


def pick_rows(field, stride, residue):
    row_count, head_count, width = field.shape
    shaped = field.reshape(row_count // stride, stride, head_count, width)
    member = (jnp.arange(stride)[:, None] == residue[None, :])[None, :, :, None]
    return jnp.sum(jnp.where(member, shaped, jnp.zeros((), field.dtype)), axis=1)


def spread_rows(level_term, stride, residue):
    peak_score, weight_sum, value_sum = level_term
    head_count, sparse_count = peak_score.shape
    member = jnp.arange(stride)[:, None] == residue[None, :]
    peak_rows = jnp.where(member[None], peak_score.T[:, None, :], NEG_FILL).reshape(
        sparse_count * stride, head_count
    )
    sum_rows = jnp.where(member[None], weight_sum.T[:, None, :], 0.0).reshape(
        sparse_count * stride, head_count
    )
    value_rows = jnp.where(member[None, :, :, None], jnp.swapaxes(value_sum, 0, 1)[:, None], 0.0)
    return (peak_rows, sum_rows, value_rows.reshape(sparse_count * stride, head_count, -1))


def combine_levels(levels):
    top_all = reduce(jnp.maximum, [level_term[0] for level_term in levels])
    numerator = 0.0
    denominator = 0.0
    for peak_score, weight_sum, value_sum in levels:
        factor = jnp.exp(peak_score - top_all)
        denominator = denominator + weight_sum * factor
        numerator = numerator + value_sum * factor[..., None]
    return numerator / denominator[..., None]


def merge_pair(earlier_part, later_part):
    top_both = jnp.maximum(earlier_part[0], later_part[0])
    factor_one = jnp.exp(earlier_part[0] - top_both)
    factor_two = jnp.exp(later_part[0] - top_both)
    weight_sum = earlier_part[1] * factor_one + later_part[1] * factor_two
    value_sum = earlier_part[2] * factor_one[..., None] + later_part[2] * factor_two[..., None]
    return (top_both, weight_sum, value_sum)


def causal_mask(query_count, key_count, offset):
    return jnp.arange(key_count)[None, :] <= (offset + jnp.arange(query_count))[:, None]


def prefill_block(pre_qkv):
    seq_index = lax.axis_index("seq")
    seq_count = lax.axis_size("seq")
    head_index = lax.axis_index(("head", "req"))
    row_count = pre_qkv.shape[0]
    width = pre_qkv.shape[2]
    head_count = width // HEAD_DIM
    head_ids = head_index * head_count + jnp.arange(head_count)
    query_rows = pre_qkv[:, 0].reshape(row_count, head_count, HEAD_DIM)
    key_rows = pre_qkv[:, 1].reshape(row_count, head_count, HEAD_DIM)
    value_rows = pre_qkv[:, 2].reshape(row_count, head_count, HEAD_DIM)
    zero_residue = jnp.zeros((head_count,), jnp.int32)
    residue_four = head_ids % 4
    residue_far = head_ids % seq_count
    block_rows = min(512, row_count)
    block_count = row_count // block_rows

    def near_part(packed):
        query_block, start_row = packed
        return partial_block(
            query_block, key_rows, value_rows, causal_mask(block_rows, row_count, start_row)
        )

    block_starts = jnp.arange(block_count, dtype=jnp.int32) * block_rows
    near_peak, near_sum, near_value = lax.map(
        near_part, (query_rows.reshape(block_count, block_rows, head_count, HEAD_DIM), block_starts)
    )
    near_term = (
        jnp.moveaxis(near_peak, 0, 1).reshape(head_count, row_count),
        jnp.moveaxis(near_sum, 0, 1).reshape(head_count, row_count),
        jnp.moveaxis(near_value, 0, 1).reshape(head_count, row_count, HEAD_DIM),
    )
    levels = [spread_rows(near_term, 1, zero_residue)]
    keys_four = pick_rows(key_rows, 4, residue_four)
    values_four = pick_rows(value_rows, 4, residue_four)
    every_keys, every_values = (
        lax.all_gather(keys_four, "seq", axis=0, tiled=True),
        lax.all_gather(values_four, "seq", axis=0, tiled=True),
    )
    start_row = seq_index // 4 * row_count
    group_keys = lax.dynamic_slice_in_dim(every_keys, start_row, row_count, 0)
    group_values = lax.dynamic_slice_in_dim(every_values, start_row, row_count, 0)
    inner_residue = residue_far // 4
    far_keys = pick_rows(every_keys, seq_count // 4, inner_residue)
    far_values = pick_rows(every_values, seq_count // 4, inner_residue)
    quarter = row_count // 4
    query_four = pick_rows(query_rows, 4, residue_four)
    mid_term = partial_block(
        query_four,
        group_keys,
        group_values,
        causal_mask(quarter, row_count, seq_index % 4 * quarter),
    )
    levels.append(spread_rows(mid_term, 4, residue_four))
    far_count = row_count // seq_count
    query_far = pick_rows(query_rows, seq_count, residue_far)
    far_term = partial_block(
        query_far, far_keys, far_values, causal_mask(far_count, row_count, seq_index * far_count)
    )
    levels.append(spread_rows(far_term, seq_count, residue_far))
    attended = combine_levels(levels)
    return attended.reshape(row_count, width).astype(jnp.bfloat16)


MESH = pl.DeviceIdType.MESH
F32 = jnp.float32
BF16 = jnp.bfloat16


def remote(source, target, send_sem, recv_sem, device):
    return pltpu.make_async_remote_copy(
        src_ref=source,
        dst_ref=target,
        send_sem=send_sem,
        recv_sem=recv_sem,
        device_id=device,
        device_id_type=MESH,
    )


def nt_dot(a, b):
    return lax.dot_general(a, b, (((1,), (1,)), ((), ())), preferred_element_type=F32)


def attend(query, parts):
    factor = HEAD_DIM ** (-0.5) * LOG2E
    scores = []
    for key, _, allowed in parts:
        block = nt_dot(query, key)
        scores.append(block if allowed is None else jnp.where(allowed, block, NEG_FILL))
    peak = reduce(jnp.maximum, [jnp.max(block, axis=1, keepdims=True) for block in scores])
    shift = peak * factor
    total = 0.0
    for block, (_, value, _) in zip(scores, parts):
        weights = jnp.exp2(block * factor - shift).astype(BF16)
        wide = jnp.concatenate([value, jnp.ones_like(value)], axis=1)
        total = total + jnp.dot(weights, wide, preferred_element_type=F32)
    weight_sum = total[:, HEAD_DIM:]
    return total[:, :HEAD_DIM] / weight_sum, shift + jnp.log2(weight_sum)


def triangle(rows):
    return lax.broadcasted_iota(jnp.int32, (rows, rows), 1) <= lax.broadcasted_iota(
        jnp.int32, (rows, rows), 0
    )


def prefill_kernel(
    qkv, out, near_o, near_l, wide, pick, kv_in, q_in, o_out, l_out, o_in, l_in,
    s_kv, r_kv, s_q, r_q, s_o, r_o, s_l, r_l,
):
    me = lax.axis_index("seq")
    row_count = qkv.shape[1]
    head_count = qkv.shape[2] // HEAD_DIM
    half = head_count // 2
    sparse = row_count // 4
    block = 256
    low, upper = pl.ds(0, half), pl.ds(half, half)

    barrier = pltpu.get_barrier_semaphore()
    for step in range(1, 4):
        pl.semaphore_signal(
            barrier, inc=1, device_id={"seq": lax.rem(me + step, 4)}, device_id_type=MESH
        )

    order = list(range(half, head_count)) + list(range(half))
    for head in order:
        lanes = pl.ds(head * HEAD_DIM, HEAD_DIM)
        for part in range(3):
            wide[...] = qkv[part, :, lanes].astype(F32)
            pick[part, head] = wide[pl.ds(head % 4, sparse, stride=4), :].astype(BF16)
    pl.semaphore_wait(barrier, 3)

    def kv_copy(heads, target):
        return remote(pick.at[pl.ds(1, 2), heads], kv_in, s_kv, r_kv, {"seq": target})

    def q_copy(heads, source, target):
        return remote(
            pick.at[0, heads], q_in.at[source - 1], s_q.at[target], r_q.at[source - 1],
            {"seq": target},
        )

    def o_copies(source, target):
        return (
            remote(
                o_out.at[target - 1], o_in.at[source], s_o.at[target - 1], r_o.at[source],
                {"seq": target},
            ),
            remote(
                l_out.at[target - 1], l_in.at[source], s_l.at[target - 1], r_l.at[source],
                {"seq": target},
            ),
        )

    sends = {
        0: [kv_copy(low, 1)],
        1: [q_copy(upper, 1, 0), kv_copy(upper, 0)],
        2: [q_copy(upper, 2, 0), q_copy(low, 2, 1), kv_copy(low, 3)],
        3: [q_copy(upper, 3, 0), q_copy(low, 3, 1), q_copy(upper, 3, 2)],
    }
    for index, copies in sends.items():

        @pl.when(me == index)
        def _(copies=copies):
            for copy in copies:
                copy.start()

    corner = triangle(block)

    def near(head):
        lanes = pl.ds(pl.multiple_of(head * HEAD_DIM, HEAD_DIM), HEAD_DIM)
        for at in range(row_count // block):
            here = pl.ds(at * block, block)
            parts = [(qkv[1, here, lanes], qkv[2, here, lanes], corner)]
            if at:
                before = pl.ds(0, at * block)
                parts.append((qkv[1, before, lanes], qkv[2, before, lanes], None))
            value, log_sum = attend(qkv[0, here, lanes], parts)
            near_o[head, here] = value
            near_l[head, here] = log_sum

    def near_heads(first, count):
        @pl.loop(first, first + count)
        def _(head):
            near(head)

    def merge(head, start, value, log_sum):
        rows = pl.ds(head % 4 + 4 * start, value.shape[0], stride=4)
        old_value, old_sum = near_o.at[head][rows, :], near_l.at[head][rows, :]
        both = log_sum + 1.0
        top = jnp.maximum(old_sum, both)
        one, two = jnp.exp2(old_sum - top), jnp.exp2(both - top)
        total = one + two
        near_o.at[head][rows, :] = (one * old_value + two * value) / total
        near_l.at[head][rows, :] = top + jnp.log2(total)

    def own_diagonal(head):
        for at in range(sparse // block):
            here = pl.ds(at * block, block)
            parts = [(pick[1, head, here], pick[2, head, here], corner)]
            if at:
                before = pl.ds(0, at * block)
                parts.append((pick[1, head, before], pick[2, head, before], None))
            merge(head, at * block, *attend(pick[0, head, here], parts))

    def serve(source, keys):
        for local in range(half):
            for at in range(sparse // block):
                here = pl.ds(at * block, block)
                value, log_sum = attend(q_in[source - 1, local, here], keys(local))
                o_out[source - 1, local, here] = value.astype(BF16)
                l_out[source - 1, local, :, here] = jnp.transpose(log_sum)[:8]

    def kept(first):
        return lambda local: [(pick[1, first + local], pick[2, first + local], None)]

    def landed(local):
        return [(kv_in[0, local], kv_in[1, local], None)]

    def extra():
        for local in range(half):
            for at in range(sparse // block):
                here = pl.ds(at * block, block)
                merge(local, at * block, *attend(pick[0, local, here], landed(local)))

    def send_back(source, target):
        for copy in o_copies(source, target):
            copy.start()

    near_heads(0, head_count)

    @pl.when(me == 0)
    def _():
        q_copy(upper, 1, 0).wait_recv()
        serve(1, kept(half))
        send_back(0, 1)
        kv_copy(upper, 0).wait_recv()
        for source in (2, 3):
            q_copy(upper, source, 0).wait_recv()
            serve(source, lambda local: kept(half)(local) + landed(local))
            send_back(0, source)

    @pl.when(me == 1)
    def _():
        kv_copy(low, 1).wait_recv()
        for source in (2, 3):
            q_copy(low, source, 1).wait_recv()
            serve(source, lambda local: kept(0)(local) + landed(local))
            send_back(1, source)
        extra()

    @pl.when(me == 2)
    def _():
        q_copy(upper, 3, 2).wait_recv()
        serve(3, kept(half))
        send_back(2, 3)

    @pl.when(me == 3)
    def _():
        kv_copy(low, 3).wait_recv()
        extra()

    for head in range(head_count):
        own_diagonal(head)

    arriving = {1: [(0, half)], 2: [(1, 0), (0, half)], 3: [(1, 0), (2, half), (0, half)]}
    for index, terms in arriving.items():

        @pl.when(me == index)
        def _(index=index, terms=terms):
            for source, first in terms:
                for copy in o_copies(source, index):
                    copy.wait_recv()
                for local in range(half):
                    rows = l_in[source, local]
                    log_sum = jnp.transpose(
                        jnp.concatenate([rows] * (HEAD_DIM // 8), axis=0)
                    )
                    merge(first + local, 0, o_in[source, local].astype(F32), log_sum)

    for head in range(head_count):
        out[:, pl.ds(head * HEAD_DIM, HEAD_DIM)] = near_o[head].astype(BF16)

    backs = {0: (1, 2, 3), 1: (2, 3), 2: (3,), 3: ()}
    for index, copies in sends.items():

        @pl.when(me == index)
        def _(index=index, copies=copies):
            for copy in copies:
                copy.wait_send()
            for target in backs[index]:
                for copy in o_copies(index, target):
                    copy.wait_send()


def prefill_fast(pre_qkv):
    qkv = jnp.moveaxis(pre_qkv, 1, 0)
    _, row_count, width = qkv.shape
    head_count = width // HEAD_DIM
    half, sparse = head_count // 2, row_count // 4
    dma = pltpu.SemaphoreType.DMA
    vmem = pltpu.VMEM
    return pl.pallas_call(
        prefill_kernel,
        out_shape=jax.ShapeDtypeStruct((row_count, width), BF16),
        in_specs=[pl.BlockSpec(memory_space=pltpu.VMEM)],
        out_specs=pl.BlockSpec(memory_space=pltpu.VMEM),
        scratch_shapes=[
            vmem((head_count, row_count, HEAD_DIM), F32),
            vmem((head_count, row_count, HEAD_DIM), F32),
            vmem((row_count, HEAD_DIM), F32),
            vmem((3, head_count, sparse, HEAD_DIM), BF16),
            vmem((2, half, sparse, HEAD_DIM), BF16),
            vmem((3, half, sparse, HEAD_DIM), BF16),
            vmem((3, half, sparse, HEAD_DIM), BF16),
            vmem((3, half, 8, sparse), F32),
            vmem((3, half, sparse, HEAD_DIM), BF16),
            vmem((3, half, 8, sparse), F32),
            dma, dma, dma((3,)), dma((3,)), dma((3,)), dma((3,)), dma((3,)), dma((3,)),
        ],
        compiler_params=pltpu.CompilerParams(
            collective_id=0, has_side_effects=True, vmem_limit_bytes=50 * 2**20
        ),
    )(qkv)


def decode_kernel(
    groups, seqs, heads,
    fresh, cache, weight, select, place, lengths, out,
    fresh_all, part_all, proj, proj_in, res_all,
    s_f, r_f, s_p, r_p, s_h, r_h, s_r, r_r,
):
    seq, head, req = lax.axis_index("seq"), lax.axis_index("head"), lax.axis_index("req")
    req_dev, _, rows_here, width = cache.shape
    head_count = width // HEAD_DIM
    items = 2 * req_dev
    columns = proj.shape[2]

    barrier = pltpu.get_barrier_semaphore()
    peers = [{"seq": lax.rem(seq + d, seqs)} for d in range(1, seqs)]
    peers += [{"head": lax.rem(head + d, heads)} for d in range(1, heads)]
    peers += [{"req": lax.rem(req + d, groups)} for d in range(1, groups)]
    for peer in peers:
        pl.semaphore_signal(barrier, inc=1, device_id=peer, device_id_type=MESH)
    pl.semaphore_wait(barrier, len(peers))

    fresh_copies = [
        remote(fresh, fresh_all.at[req], s_f.at[d - 1], r_f.at[d - 1],
               {"req": lax.rem(req + d, groups)})
        for d in range(1, groups)
    ]
    for copy in fresh_copies:
        copy.start()
    fresh_all[req] = fresh[...]
    for copy in fresh_copies:
        copy.wait_recv()

    def chosen(part):
        total = 0.0
        for group in range(groups):
            total = total + jnp.dot(select[group], fresh_all[group, part], preferred_element_type=F32)
        return total

    queries = chosen(0)
    new_keys, new_values = chosen(1).astype(BF16), chosen(2).astype(BF16)
    big = 2 * head_count
    row = lax.broadcasted_iota(jnp.int32, (big, width), 0)
    lane = lax.broadcasted_iota(jnp.int32, (big, width), 1)
    own_head = lax.rem(row, head_count) == lane // HEAD_DIM
    factor = HEAD_DIM ** (-0.5) * LOG2E
    new_col = lax.broadcasted_iota(jnp.int32, (big, items), 1)
    new_row = lax.broadcasted_iota(jnp.int32, (big, items), 0)
    key_at = lax.broadcasted_iota(jnp.int32, (big, rows_here), 1) + seq * rows_here
    for item in range(req_dev):
        tiled = jnp.concatenate(
            [
                jnp.broadcast_to(queries[2 * item + t : 2 * item + t + 1], (head_count, width))
                for t in range(2)
            ],
            axis=0,
        )
        spread = jnp.where(own_head, tiled, 0.0).astype(BF16)
        old = key_at < lengths[req * req_dev + item]
        recent = (new_col >= 2 * item) & (new_col <= 2 * item + new_row // head_count) & (seq == 0)
        scores = jnp.where(old, nt_dot(spread, cache[item, 0]) * factor, NEG_FILL)
        new_scores = jnp.where(recent, nt_dot(spread, new_keys) * factor, NEG_FILL)
        peak = jnp.maximum(
            jnp.max(scores, axis=1, keepdims=True), jnp.max(new_scores, axis=1, keepdims=True)
        )
        weights = jnp.where(old, jnp.exp2(scores - peak), 0.0)
        new_weights = jnp.where(recent, jnp.exp2(new_scores - peak), 0.0)
        weight_sum = jnp.sum(weights, axis=1, keepdims=True) + jnp.sum(
            new_weights, axis=1, keepdims=True
        )
        value = jnp.dot(
            weights.astype(BF16), cache[item, 1], preferred_element_type=F32
        ) + jnp.dot(new_weights.astype(BF16), new_values, preferred_element_type=F32)
        for kind, field in enumerate((peak, weight_sum, value)):
            kept = jnp.where(own_head, field, 0.0)
            for t in range(2):
                part_all[seq, kind, pl.ds(2 * item + t, 1)] = jnp.sum(
                    kept[t * head_count : (t + 1) * head_count], axis=0, keepdims=True
                )

    part_copies = [
        remote(part_all.at[seq], part_all.at[seq], s_p.at[d - 1], r_p.at[d - 1],
               {"seq": lax.rem(seq + d, seqs)})
        for d in range(1, seqs)
    ]
    for copy in part_copies:
        copy.start()
    for copy in part_copies:
        copy.wait_recv()
    top = reduce(jnp.maximum, [part_all[at, 0] for at in range(seqs)])
    numerator, denominator = 0.0, 0.0
    for at in range(seqs):
        scale = jnp.exp2(part_all[at, 0] - top)
        denominator = denominator + scale * part_all[at, 1]
        numerator = numerator + scale * part_all[at, 2]
    mixed = (numerator / denominator).astype(BF16)
    projected = jnp.dot(mixed, weight[...], preferred_element_type=F32)
    projected = jnp.concatenate([projected, jnp.zeros_like(projected)], axis=0).astype(BF16)
    for at in range(heads):
        proj[at] = projected[:, at * columns : (at + 1) * columns]

    head_copies = []
    for d in range(1, heads):
        target = lax.rem(head + d, heads)
        head_copies.append(
            remote(proj.at[target], proj_in.at[d - 1], s_h.at[d - 1], r_h.at[d - 1], {"head": target})
        )
    for copy in head_copies:
        copy.start()
    total = proj[head].astype(F32)
    for copy in head_copies:
        copy.wait_recv()
    for d in range(1, heads):
        total = total + proj_in[d - 1].astype(F32)
    res_all[req] = total.astype(BF16)

    res_copies = [
        remote(res_all.at[req], res_all.at[req], s_r.at[d - 1], r_r.at[d - 1],
               {"req": lax.rem(req + d, groups)})
        for d in range(1, groups)
    ]
    for copy in res_copies:
        copy.start()
    for copy in res_copies:
        copy.wait_recv()
    final = 0.0
    for group in range(groups):
        final = final + jnp.dot(place[group], res_all[group], preferred_element_type=F32)
    out[...] = final.astype(BF16)
    for copy in fresh_copies + part_copies + head_copies + res_copies:
        copy.wait_send()


def decode_fast(cache_kv, dec_new, out_weight, owner_slot, prompt_lengths, mesh_shape):
    seqs, heads, groups = mesh_shape["seq"], mesh_shape["head"], mesh_shape["req"]
    req_dev, _, rows_here, width = cache_kv.shape
    slot_dev = dec_new.shape[0]
    rows = 2 * slot_dev
    items = 2 * req_dev
    columns = out_weight.shape[1] // heads
    req = lax.axis_index("req")
    fresh = jnp.transpose(dec_new, (1, 0, 2, 3)).reshape(3, rows, width)
    owners = owner_slot.reshape(groups, req_dev)
    item_slot = (owners[:, :, None] * 2 + jnp.arange(2)).reshape(groups, items)
    here = lax.dynamic_index_in_dim(item_slot, req, 0, keepdims=False)
    every = (jnp.arange(groups) * rows)[:, None, None] + jnp.arange(rows)[None, None, :]
    select = (here[None, :, None] == every).astype(BF16)
    filled = jnp.concatenate([item_slot, jnp.full((groups, items), -1, jnp.int32)], axis=1)
    place = (
        filled[:, None, :] == (req * rows + jnp.arange(rows))[None, :, None]
    ).astype(BF16)
    dma = pltpu.SemaphoreType.DMA
    vmem = pltpu.VMEM
    whole = pl.BlockSpec(memory_space=pltpu.VMEM)
    out = pl.pallas_call(
        functools.partial(decode_kernel, groups, seqs, heads),
        out_shape=jax.ShapeDtypeStruct((rows, columns), BF16),
        in_specs=[whole] * 5 + [pl.BlockSpec(memory_space=pltpu.SMEM)],
        out_specs=whole,
        scratch_shapes=[
            vmem((groups, 3, rows, width), BF16),
            vmem((seqs, 3, items, width), F32),
            vmem((heads, 2 * items, columns), BF16),
            vmem((heads - 1, 2 * items, columns), BF16),
            vmem((groups, 2 * items, columns), BF16),
            dma((groups - 1,)), dma((groups - 1,)),
            dma((seqs - 1,)), dma((seqs - 1,)),
            dma((heads - 1,)), dma((heads - 1,)),
            dma((groups - 1,)), dma((groups - 1,)),
        ],
        compiler_params=pltpu.CompilerParams(
            collective_id=1, has_side_effects=True, vmem_limit_bytes=32 * 2**20
        ),
    )(fresh, cache_kv, out_weight, select, place, prompt_lengths)
    return out.reshape(slot_dev, 2, columns)


def on_device(mesh_shape, pre_qkv, cache_kv, dec_new, out_weight, owner_slot, prompt_lengths):
    head_count = pre_qkv.shape[2] // HEAD_DIM
    plain = mesh_shape["seq"] != 4 or head_count % 4
    decode_out = decode_fast(
        cache_kv, dec_new, out_weight, owner_slot, prompt_lengths, mesh_shape
    )
    prefill_out = prefill_block(pre_qkv) if plain else prefill_fast(pre_qkv)
    return (prefill_out, decode_out)


def solution(mesh):
    return jax.shard_map(
        functools.partial(on_device, dict(mesh.shape)),
        mesh=mesh,
        in_specs=(
            P("seq", None, ("head", "req")),
            P("req", None, "seq", "head"),
            P("req", None, None, "head"),
            P("head", "seq"),
            P(),
            P(),
        ),
        out_specs=(P("seq", ("head", "req")), P("req", None, ("seq", "head"))),
        check_vma=False,
    )
```

```python
import functools
from functools import reduce

import jax
import jax.numpy as jnp
from jax import lax
from jax.experimental import pallas as pl
from jax.experimental.pallas import tpu as pltpu
from jax.sharding import PartitionSpec as P

HEAD_DIM = 128
LOG2E = 1.4426950408889634


NEG_FILL = -1e30


def merged_2(value, axis, join):
    pieces = jax.tree.map(lambda part: lax.all_gather(part, axis), value)
    head = jax.tree.map(lambda part: part[0], pieces)
    tail = jax.tree.map(lambda part: part[1:], pieces)
    total, _ = lax.scan(lambda total, section: (join(total, section), None), head, tail)
    return total


def partial_block(query_rows, key_rows, value_rows, allowed):
    score_scale = query_rows.shape[-1] ** (-0.5)
    scores = (
        jnp.einsum("qhd,khd->hqk", query_rows, key_rows, preferred_element_type=jnp.float32)
        * score_scale
    )
    scores = jnp.where(allowed, scores, NEG_FILL)
    peak_score = jnp.max(scores, axis=-1)
    weights = jnp.where(allowed, jnp.exp(scores - peak_score[..., None]), 0.0)
    weight_sum = jnp.sum(weights, axis=-1)
    value_sum = jnp.einsum(
        "hqk,khd->hqd", weights.astype(jnp.bfloat16), value_rows, preferred_element_type=jnp.float32
    )
    return (peak_score, weight_sum, value_sum)


def pick_rows(field, stride, residue):
    row_count, head_count, width = field.shape
    shaped = field.reshape(row_count // stride, stride, head_count, width)
    member = (jnp.arange(stride)[:, None] == residue[None, :])[None, :, :, None]
    return jnp.sum(jnp.where(member, shaped, jnp.zeros((), field.dtype)), axis=1)


def spread_rows(level_term, stride, residue):
    peak_score, weight_sum, value_sum = level_term
    head_count, sparse_count = peak_score.shape
    member = jnp.arange(stride)[:, None] == residue[None, :]
    peak_rows = jnp.where(member[None], peak_score.T[:, None, :], NEG_FILL).reshape(
        sparse_count * stride, head_count
    )
    sum_rows = jnp.where(member[None], weight_sum.T[:, None, :], 0.0).reshape(
        sparse_count * stride, head_count
    )
    value_rows = jnp.where(member[None, :, :, None], jnp.swapaxes(value_sum, 0, 1)[:, None], 0.0)
    return (peak_rows, sum_rows, value_rows.reshape(sparse_count * stride, head_count, -1))


def combine_levels(levels):
    top_all = reduce(jnp.maximum, [level_term[0] for level_term in levels])
    numerator = 0.0
    denominator = 0.0
    for peak_score, weight_sum, value_sum in levels:
        factor = jnp.exp(peak_score - top_all)
        denominator = denominator + weight_sum * factor
        numerator = numerator + value_sum * factor[..., None]
    return numerator / denominator[..., None]


def merge_pair(earlier_part, later_part):
    top_both = jnp.maximum(earlier_part[0], later_part[0])
    factor_one = jnp.exp(earlier_part[0] - top_both)
    factor_two = jnp.exp(later_part[0] - top_both)
    weight_sum = earlier_part[1] * factor_one + later_part[1] * factor_two
    value_sum = earlier_part[2] * factor_one[..., None] + later_part[2] * factor_two[..., None]
    return (top_both, weight_sum, value_sum)


def causal_mask(query_count, key_count, offset):
    return jnp.arange(key_count)[None, :] <= (offset + jnp.arange(query_count))[:, None]


def prefill_block(pre_qkv):
    seq_index = lax.axis_index("seq")
    seq_count = lax.axis_size("seq")
    head_index = lax.axis_index(("head", "req"))
    row_count = pre_qkv.shape[0]
    width = pre_qkv.shape[2]
    head_count = width // HEAD_DIM
    head_ids = head_index * head_count + jnp.arange(head_count)
    query_rows = pre_qkv[:, 0].reshape(row_count, head_count, HEAD_DIM)
    key_rows = pre_qkv[:, 1].reshape(row_count, head_count, HEAD_DIM)
    value_rows = pre_qkv[:, 2].reshape(row_count, head_count, HEAD_DIM)
    zero_residue = jnp.zeros((head_count,), jnp.int32)
    residue_four = head_ids % 4
    residue_far = head_ids % seq_count
    block_rows = min(512, row_count)
    block_count = row_count // block_rows

    def near_part(packed):
        query_block, start_row = packed
        return partial_block(
            query_block, key_rows, value_rows, causal_mask(block_rows, row_count, start_row)
        )

    block_starts = jnp.arange(block_count, dtype=jnp.int32) * block_rows
    near_peak, near_sum, near_value = lax.map(
        near_part, (query_rows.reshape(block_count, block_rows, head_count, HEAD_DIM), block_starts)
    )
    near_term = (
        jnp.moveaxis(near_peak, 0, 1).reshape(head_count, row_count),
        jnp.moveaxis(near_sum, 0, 1).reshape(head_count, row_count),
        jnp.moveaxis(near_value, 0, 1).reshape(head_count, row_count, HEAD_DIM),
    )
    levels = [spread_rows(near_term, 1, zero_residue)]
    keys_four = pick_rows(key_rows, 4, residue_four)
    values_four = pick_rows(value_rows, 4, residue_four)
    every_keys, every_values = (
        lax.all_gather(keys_four, "seq", axis=0, tiled=True),
        lax.all_gather(values_four, "seq", axis=0, tiled=True),
    )
    start_row = seq_index // 4 * row_count
    group_keys = lax.dynamic_slice_in_dim(every_keys, start_row, row_count, 0)
    group_values = lax.dynamic_slice_in_dim(every_values, start_row, row_count, 0)
    inner_residue = residue_far // 4
    far_keys = pick_rows(every_keys, seq_count // 4, inner_residue)
    far_values = pick_rows(every_values, seq_count // 4, inner_residue)
    quarter = row_count // 4
    query_four = pick_rows(query_rows, 4, residue_four)
    mid_term = partial_block(
        query_four,
        group_keys,
        group_values,
        causal_mask(quarter, row_count, seq_index % 4 * quarter),
    )
    levels.append(spread_rows(mid_term, 4, residue_four))
    far_count = row_count // seq_count
    query_far = pick_rows(query_rows, seq_count, residue_far)
    far_term = partial_block(
        query_far, far_keys, far_values, causal_mask(far_count, row_count, seq_index * far_count)
    )
    levels.append(spread_rows(far_term, seq_count, residue_far))
    attended = combine_levels(levels)
    return attended.reshape(row_count, width).astype(jnp.bfloat16)


MESH = pl.DeviceIdType.MESH
F32 = jnp.float32
BF16 = jnp.bfloat16


def remote(source, target, send_sem, recv_sem, device):
    return pltpu.make_async_remote_copy(
        src_ref=source,
        dst_ref=target,
        send_sem=send_sem,
        recv_sem=recv_sem,
        device_id=device,
        device_id_type=MESH,
    )


def nt_dot(a, b):
    return lax.dot_general(a, b, (((1,), (1,)), ((), ())), preferred_element_type=F32)


def attend_all(jobs):
    factor = HEAD_DIM ** (-0.5) * LOG2E

    def scores_of(job):
        query, parts, _ = job()
        scores = []
        for key, _, allowed in parts:
            block = nt_dot(query, key)
            scores.append(block if allowed is None else jnp.where(allowed, block, NEG_FILL))
        return scores

    def finish(job, scores):
        _, parts, done = job()
        peak = reduce(jnp.maximum, [jnp.max(block, axis=1, keepdims=True) for block in scores])
        shift = peak * factor
        total = 0.0
        for block, (_, value, _) in zip(scores, parts):
            weights = jnp.exp2(block * factor - shift).astype(BF16)
            wide = jnp.concatenate([value, jnp.ones_like(value)], axis=1)
            total = total + jnp.dot(weights, wide, preferred_element_type=F32)
        weight_sum = total[:, HEAD_DIM:]
        done(total[:, :HEAD_DIM] / weight_sum, shift + jnp.log2(weight_sum))

    scores = scores_of(jobs[0])
    for at, job in enumerate(jobs):
        later = scores_of(jobs[at + 1]) if at + 1 < len(jobs) else None
        finish(job, scores)
        scores = later


def triangle(rows):
    return lax.broadcasted_iota(jnp.int32, (rows, rows), 1) <= lax.broadcasted_iota(
        jnp.int32, (rows, rows), 0
    )


def joint_kernel(
    groups, heads, qkv, fresh, cache, weight, select, place, lengths, out, decode_out, near_o, near_l, wide, pick, kv_in, q_in, o_out, l_out, o_in, l_in,
    s_kv, r_kv, s_q, r_q, s_o, r_o, s_l, r_l, *decode_scratch,
):
    me = lax.axis_index("seq")
    row_count = qkv.shape[1]
    head_count = qkv.shape[2] // HEAD_DIM
    half = head_count // 2
    sparse = row_count // 4
    block = 256
    low, upper = pl.ds(0, half), pl.ds(half, half)

    all_here = greet(4, heads, groups)
    decode = decode_steps(
        groups, 4, heads, fresh, cache, weight, select, place, lengths, decode_out, *decode_scratch
    )

    order = list(range(half, head_count)) + list(range(half))
    for head in order:
        lanes = pl.ds(head * HEAD_DIM, HEAD_DIM)
        for part in range(3):
            wide[...] = qkv[part, :, lanes].astype(F32)
            pick[part, head] = wide[pl.ds(head % 4, sparse, stride=4), :].astype(BF16)
    all_here()

    def kv_copy(heads, target):
        return remote(pick.at[pl.ds(1, 2), heads], kv_in, s_kv, r_kv, {"seq": target})

    def q_copy(heads, source, target):
        return remote(
            pick.at[0, heads], q_in.at[source - 1], s_q.at[target], r_q.at[source - 1],
            {"seq": target},
        )

    def o_copies(source, target):
        return (
            remote(
                o_out.at[target - 1], o_in.at[source], s_o.at[target - 1], r_o.at[source],
                {"seq": target},
            ),
            remote(
                l_out.at[target - 1], l_in.at[source], s_l.at[target - 1], r_l.at[source],
                {"seq": target},
            ),
        )

    sends = {
        0: [kv_copy(low, 1)],
        1: [q_copy(upper, 1, 0), kv_copy(upper, 0)],
        2: [q_copy(upper, 2, 0), q_copy(low, 2, 1), kv_copy(low, 3)],
        3: [q_copy(upper, 3, 0), q_copy(low, 3, 1), q_copy(upper, 3, 2)],
    }
    for index, copies in sends.items():

        @pl.when(me == index)
        def _(copies=copies):
            for copy in copies:
                copy.start()

    next(decode)
    corner = triangle(block)

    def near(head):
        lanes = pl.ds(pl.multiple_of(head * HEAD_DIM, HEAD_DIM), HEAD_DIM)

        def job(at):
            here = pl.ds(at * block, block)
            parts = [(qkv[1, here, lanes], qkv[2, here, lanes], corner)]
            if at:
                before = pl.ds(0, at * block)
                parts.append((qkv[1, before, lanes], qkv[2, before, lanes], None))

            def done(value, log_sum):
                near_o[head, here] = value
                near_l[head, here] = log_sum

            return qkv[0, here, lanes], parts, done

        attend_all([functools.partial(job, at) for at in range(row_count // block)])

    def near_heads(first, count):
        @pl.loop(first, first + count)
        def _(head):
            near(head)

    def merge(head, start, value, log_sum):
        rows = pl.ds(head % 4 + 4 * start, value.shape[0], stride=4)
        old_value, old_sum = near_o.at[head][rows, :], near_l.at[head][rows, :]
        both = log_sum + 1.0
        top = jnp.maximum(old_sum, both)
        one, two = jnp.exp2(old_sum - top), jnp.exp2(both - top)
        total = one + two
        near_o.at[head][rows, :] = (one * old_value + two * value) / total
        near_l.at[head][rows, :] = top + jnp.log2(total)

    def own_diagonal():
        def job(head, at):
            here = pl.ds(at * block, block)
            parts = [(pick[1, head, here], pick[2, head, here], corner)]
            if at:
                before = pl.ds(0, at * block)
                parts.append((pick[1, head, before], pick[2, head, before], None))
            return pick[0, head, here], parts, functools.partial(merge, head, at * block)

        attend_all(
            [functools.partial(job, h, at) for h in range(head_count) for at in range(sparse // block)]
        )

    def serve(source, keys):
        def job(local, at):
            here = pl.ds(at * block, block)

            def done(value, log_sum):
                o_out[source - 1, local, here] = value.astype(BF16)
                l_out[source - 1, local, :, here] = jnp.transpose(log_sum)[:8]

            return q_in[source - 1, local, here], keys(local), done

        attend_all(
            [functools.partial(job, local, at) for local in range(half) for at in range(sparse // block)]
        )

    def kept(first):
        return lambda local: [(pick[1, first + local], pick[2, first + local], None)]

    def landed(local):
        return [(kv_in[0, local], kv_in[1, local], None)]

    def extra():
        def job(local, at):
            here = pl.ds(at * block, block)
            return pick[0, local, here], landed(local), functools.partial(merge, local, at * block)

        attend_all(
            [functools.partial(job, local, at) for local in range(half) for at in range(sparse // block)]
        )

    def send_back(source, target):
        for copy in o_copies(source, target):
            copy.start()

    near_heads(0, half)
    next(decode)

    @pl.when(me == 0)
    def _():
        q_copy(upper, 1, 0).wait_recv()
        serve(1, kept(half))
        send_back(0, 1)
        kv_copy(upper, 0).wait_recv()

    @pl.when(me == 1)
    def _():
        kv_copy(low, 1).wait_recv()

    @pl.when(me == 2)
    def _():
        q_copy(upper, 3, 2).wait_recv()
        serve(3, kept(half))
        send_back(2, 3)

    @pl.when(me == 3)
    def _():
        kv_copy(low, 3).wait_recv()

    next(decode)
    for index, heads_here, first in ((0, upper, half), (1, low, 0)):

        @pl.when(me == index)
        def _(index=index, heads_here=heads_here, first=first):
            for source in (2, 3):
                q_copy(heads_here, source, index).wait_recv()
                serve(source, lambda local: kept(first)(local) + landed(local))
                send_back(index, source)

    @pl.when(me % 2 == 1)
    def _():
        extra()

    next(decode)
    near_heads(half, half)
    next(decode)

    own_diagonal()

    arriving = {1: [(0, half)], 2: [(1, 0), (0, half)], 3: [(1, 0), (2, half), (0, half)]}
    for index, terms in arriving.items():

        @pl.when(me == index)
        def _(index=index, terms=terms):
            for source, first in terms:
                for copy in o_copies(source, index):
                    copy.wait_recv()
                for local in range(half):
                    rows = l_in[source, local]
                    log_sum = jnp.transpose(
                        jnp.concatenate([rows] * (HEAD_DIM // 8), axis=0)
                    )
                    merge(first + local, 0, o_in[source, local].astype(F32), log_sum)

    for head in range(head_count):
        out[:, pl.ds(head * HEAD_DIM, HEAD_DIM)] = near_o[head].astype(BF16)

    backs = {0: (1, 2, 3), 1: (2, 3), 2: (3,), 3: ()}
    for index, copies in sends.items():

        @pl.when(me == index)
        def _(index=index, copies=copies):
            for copy in copies:
                copy.wait_send()
            for target in backs[index]:
                for copy in o_copies(index, target):
                    copy.wait_send()
    next(decode, None)


def greet(seqs, heads, groups):
    seq, head, req = lax.axis_index("seq"), lax.axis_index("head"), lax.axis_index("req")
    peers = [{"seq": lax.rem(seq + d, seqs)} for d in range(1, seqs)]
    peers += [{"head": lax.rem(head + d, heads)} for d in range(1, heads)]
    peers += [{"req": lax.rem(req + d, groups)} for d in range(1, groups)]
    barrier = pltpu.get_barrier_semaphore()
    for peer in peers:
        pl.semaphore_signal(barrier, inc=1, device_id=peer, device_id_type=MESH)
    return lambda: pl.semaphore_wait(barrier, len(peers))


def decode_kernel(groups, seqs, heads, *refs):
    greet(seqs, heads, groups)()
    for _ in decode_steps(groups, seqs, heads, *refs):
        pass


def decode_steps(
    groups, seqs, heads,
    fresh, cache, weight, select, place, lengths, out,
    fresh_all, part_all, proj, proj_in, res_all,
    s_f, r_f, s_p, r_p, s_h, r_h, s_r, r_r,
):
    seq, head, req = lax.axis_index("seq"), lax.axis_index("head"), lax.axis_index("req")
    req_dev, _, rows_here, width = cache.shape
    head_count = width // HEAD_DIM
    items = 2 * req_dev
    columns = proj.shape[2]

    fresh_copies = [
        remote(fresh, fresh_all.at[req], s_f.at[d - 1], r_f.at[d - 1],
               {"req": lax.rem(req + d, groups)})
        for d in range(1, groups)
    ]
    for copy in fresh_copies:
        copy.start()
    fresh_all[req] = fresh[...]
    yield
    for copy in fresh_copies:
        copy.wait_recv()

    def chosen(part):
        total = 0.0
        for group in range(groups):
            total = total + jnp.dot(select[group], fresh_all[group, part], preferred_element_type=F32)
        return total

    queries = chosen(0)
    new_keys, new_values = chosen(1).astype(BF16), chosen(2).astype(BF16)
    big = 2 * head_count
    row = lax.broadcasted_iota(jnp.int32, (big, width), 0)
    lane = lax.broadcasted_iota(jnp.int32, (big, width), 1)
    own_head = lax.rem(row, head_count) == lane // HEAD_DIM
    factor = HEAD_DIM ** (-0.5) * LOG2E
    new_col = lax.broadcasted_iota(jnp.int32, (big, items), 1)
    new_row = lax.broadcasted_iota(jnp.int32, (big, items), 0)
    key_at = lax.broadcasted_iota(jnp.int32, (big, rows_here), 1) + seq * rows_here
    for item in range(req_dev):
        tiled = jnp.concatenate(
            [
                jnp.broadcast_to(queries[2 * item + t : 2 * item + t + 1], (head_count, width))
                for t in range(2)
            ],
            axis=0,
        )
        spread = jnp.where(own_head, tiled, 0.0).astype(BF16)
        old = key_at < lengths[req * req_dev + item]
        recent = (new_col >= 2 * item) & (new_col <= 2 * item + new_row // head_count) & (seq == 0)
        scores = jnp.where(old, nt_dot(spread, cache[item, 0]) * factor, NEG_FILL)
        new_scores = jnp.where(recent, nt_dot(spread, new_keys) * factor, NEG_FILL)
        peak = jnp.maximum(
            jnp.max(scores, axis=1, keepdims=True), jnp.max(new_scores, axis=1, keepdims=True)
        )
        weights = jnp.where(old, jnp.exp2(scores - peak), 0.0)
        new_weights = jnp.where(recent, jnp.exp2(new_scores - peak), 0.0)
        weight_sum = jnp.sum(weights, axis=1, keepdims=True) + jnp.sum(
            new_weights, axis=1, keepdims=True
        )
        value = jnp.dot(
            weights.astype(BF16), cache[item, 1], preferred_element_type=F32
        ) + jnp.dot(new_weights.astype(BF16), new_values, preferred_element_type=F32)
        for kind, field in enumerate((peak, weight_sum, value)):
            kept = jnp.where(own_head, field, 0.0)
            for t in range(2):
                part_all[seq, kind, pl.ds(2 * item + t, 1)] = jnp.sum(
                    kept[t * head_count : (t + 1) * head_count], axis=0, keepdims=True
                )

    part_copies = [
        remote(part_all.at[seq], part_all.at[seq], s_p.at[d - 1], r_p.at[d - 1],
               {"seq": lax.rem(seq + d, seqs)})
        for d in range(1, seqs)
    ]
    for copy in part_copies:
        copy.start()
    yield
    for copy in part_copies:
        copy.wait_recv()
    top = reduce(jnp.maximum, [part_all[at, 0] for at in range(seqs)])
    numerator, denominator = 0.0, 0.0
    for at in range(seqs):
        scale = jnp.exp2(part_all[at, 0] - top)
        denominator = denominator + scale * part_all[at, 1]
        numerator = numerator + scale * part_all[at, 2]
    mixed = (numerator / denominator).astype(BF16)
    projected = jnp.dot(mixed, weight[...], preferred_element_type=F32)
    projected = jnp.concatenate([projected, jnp.zeros_like(projected)], axis=0).astype(BF16)
    for at in range(heads):
        proj[at] = projected[:, at * columns : (at + 1) * columns]

    head_copies = []
    for d in range(1, heads):
        target = lax.rem(head + d, heads)
        head_copies.append(
            remote(proj.at[target], proj_in.at[d - 1], s_h.at[d - 1], r_h.at[d - 1], {"head": target})
        )
    for copy in head_copies:
        copy.start()
    yield
    total = proj[head].astype(F32)
    for copy in head_copies:
        copy.wait_recv()
    for d in range(1, heads):
        total = total + proj_in[d - 1].astype(F32)
    res_all[req] = total.astype(BF16)

    res_copies = [
        remote(res_all.at[req], res_all.at[req], s_r.at[d - 1], r_r.at[d - 1],
               {"req": lax.rem(req + d, groups)})
        for d in range(1, groups)
    ]
    for copy in res_copies:
        copy.start()
    yield
    for copy in res_copies:
        copy.wait_recv()
    final = 0.0
    for group in range(groups):
        final = final + jnp.dot(place[group], res_all[group], preferred_element_type=F32)
    out[...] = final.astype(BF16)
    yield
    for copy in fresh_copies + part_copies + head_copies + res_copies:
        copy.wait_send()


def run_kernels(pre_qkv, plain, cache_kv, dec_new, out_weight, owner_slot, prompt_lengths, mesh_shape):
    seqs, heads, groups = mesh_shape["seq"], mesh_shape["head"], mesh_shape["req"]
    req_dev, _, rows_here, width = cache_kv.shape
    slot_dev = dec_new.shape[0]
    rows = 2 * slot_dev
    items = 2 * req_dev
    columns = out_weight.shape[1] // heads
    req = lax.axis_index("req")
    fresh = jnp.transpose(dec_new, (1, 0, 2, 3)).reshape(3, rows, width)
    owners = owner_slot.reshape(groups, req_dev)
    item_slot = (owners[:, :, None] * 2 + jnp.arange(2)).reshape(groups, items)
    here = lax.dynamic_index_in_dim(item_slot, req, 0, keepdims=False)
    every = (jnp.arange(groups) * rows)[:, None, None] + jnp.arange(rows)[None, None, :]
    select = (here[None, :, None] == every).astype(BF16)
    filled = jnp.concatenate([item_slot, jnp.full((groups, items), -1, jnp.int32)], axis=1)
    place = (
        filled[:, None, :] == (req * rows + jnp.arange(rows))[None, :, None]
    ).astype(BF16)
    dma = pltpu.SemaphoreType.DMA
    vmem = pltpu.VMEM
    whole = pl.BlockSpec(memory_space=pltpu.VMEM)
    smem = pl.BlockSpec(memory_space=pltpu.SMEM)
    operands = (fresh, cache_kv, out_weight, select, place, prompt_lengths)
    decode_shape = jax.ShapeDtypeStruct((rows, columns), BF16)
    decode_scratch = [
        vmem((groups, 3, rows, width), BF16),
        vmem((seqs, 3, items, width), F32),
        vmem((heads, 2 * items, columns), BF16),
        vmem((heads - 1, 2 * items, columns), BF16),
        vmem((groups, 2 * items, columns), BF16),
    ]
    for peers in (groups, seqs, heads, groups):
        decode_scratch += [dma((peers - 1,)), dma((peers - 1,))]
    if plain:
        out = pl.pallas_call(
            functools.partial(decode_kernel, groups, seqs, heads),
            out_shape=decode_shape,
            in_specs=[whole] * 5 + [smem],
            out_specs=whole,
            scratch_shapes=decode_scratch,
            compiler_params=pltpu.CompilerParams(
                collective_id=0, has_side_effects=True, vmem_limit_bytes=32 * 2**20
            ),
        )(*operands)
        return prefill_block(pre_qkv), out.reshape(slot_dev, 2, columns)
    qkv = jnp.moveaxis(pre_qkv, 1, 0)
    _, row_count, pre_width = qkv.shape
    head_count = pre_width // HEAD_DIM
    half, sparse = head_count // 2, row_count // 4
    prefill_out, out = pl.pallas_call(
        functools.partial(joint_kernel, groups, heads),
        out_shape=(jax.ShapeDtypeStruct((row_count, pre_width), BF16), decode_shape),
        in_specs=[whole] * 6 + [smem],
        out_specs=(whole, whole),
        scratch_shapes=[
            vmem((head_count, row_count, HEAD_DIM), F32),
            vmem((head_count, row_count, HEAD_DIM), F32),
            vmem((row_count, HEAD_DIM), F32),
            vmem((3, head_count, sparse, HEAD_DIM), BF16),
            vmem((2, half, sparse, HEAD_DIM), BF16),
            vmem((3, half, sparse, HEAD_DIM), BF16),
            vmem((3, half, sparse, HEAD_DIM), BF16),
            vmem((3, half, 8, sparse), F32),
            vmem((3, half, sparse, HEAD_DIM), BF16),
            vmem((3, half, 8, sparse), F32),
            dma, dma, dma((3,)), dma((3,)), dma((3,)), dma((3,)), dma((3,)), dma((3,)),
            *decode_scratch,
        ],
        compiler_params=pltpu.CompilerParams(
            collective_id=0, has_side_effects=True, vmem_limit_bytes=54 * 2**20
        ),
    )(qkv, *operands)
    return prefill_out, out.reshape(slot_dev, 2, columns)


def on_device(mesh_shape, pre_qkv, cache_kv, dec_new, out_weight, owner_slot, prompt_lengths):
    head_count = pre_qkv.shape[2] // HEAD_DIM
    plain = mesh_shape["seq"] != 4 or head_count % 4
    return run_kernels(
        pre_qkv, plain, cache_kv, dec_new, out_weight, owner_slot, prompt_lengths, mesh_shape
    )


def solution(mesh):
    return jax.shard_map(
        functools.partial(on_device, dict(mesh.shape)),
        mesh=mesh,
        in_specs=(
            P("seq", None, ("head", "req")),
            P("req", None, "seq", "head"),
            P("req", None, None, "head"),
            P("head", "seq"),
            P(),
            P(),
        ),
        out_specs=(P("seq", ("head", "req")), P("req", None, ("seq", "head"))),
        check_vma=False,
    )
```
